32 devices in a mesh: rep: 8 (over y, x, core), ep: 4 (over z).
Axes of the slice: x: 2, y: 2, z: 4, core: 2. Of those that a mesh axis runs over, the one named last changes fastest.
Arguments:
- inputs: bfloat16 [4096, 2048], P(('rep', 'ep')), may hold values from -6 to 6
- out_grad: bfloat16 [4096, 2048], P(('rep', 'ep')), may hold values from -6 to 6
- routes: int32 [4096, 8], P(('rep', 'ep')), may hold values from 0 to 127, as said below
- gate_probs: float32 [4096, 8], P(('rep', 'ep')), may hold values from 0.05 to 0.6
- gate_weight: bfloat16 [4, 2048, 768], P('ep'), may hold values from -0.125 to 0.125
- up_weight: bfloat16 [4, 2048, 768], P('ep'), may hold values from -0.125 to 0.125
- down_weight: bfloat16 [4, 768, 2048], P('ep'), may hold values from -0.21875 to 0.21875
Outputs:
- input_grad: bfloat16 [4096, 2048], P(('rep', 'ep'))
- gate_grad: float32 [4, 2048, 768], P('ep', 'rep')
- up_grad: float32 [4, 2048, 768], P('ep', 'rep')
- down_update: float32 [4, 2048, 768], P('ep', 'rep')
The draws below stay inside these ranges and needn't reach their ends.
Inputs may be any that keep to these rules, and one draw needn't show every extreme that they name: `routes`: each row names 8 different experts. Among the rows of one device (aligned blocks of 128 rows), each computed expert (0 to 3) is named by at most 16 rows, and in every group of devices along ep one computed expert is named by exactly 16 rows of every device of the group.
All inputs are finite; a program needn't handle non-finite values.
Results may differ from the reference program's by a relative error of at most 0.0057.
Values may be sent and summed in bfloat16 or wider, within the bound.
A program may use at most 128 MiB of HBM per device.

```python
import math
import jax
import jax.numpy as jnp
from jax import lax

D = 2048
F = 768
EXPERTS = 128
TOPK = 8
ITERS = 3
TOK_DEV = 128
CAP = 16
WINDOW = 4
GROUPS = 8
TOKENS = 4096


def draw_routes(key, part):
    key = jax.random.fold_in(key, 11)
    blocks = TOKENS // TOK_DEV
    key_hot, key_count, key_order, key_slot, key_step, key_score = jax.random.split(key, 6)
    hot = jax.random.randint(key_hot, (blocks // WINDOW,), 0, WINDOW)
    hot_block = jnp.repeat(hot, WINDOW)
    labels = jnp.arange(WINDOW, dtype=jnp.int32)
    counts = jax.random.randint(key_count, (blocks, WINDOW), 1, CAP)
    counts = jnp.where(labels[None, :] == hot_block[:, None], CAP, counts)
    ends = jnp.cumsum(counts, axis=1)
    starts = ends - counts
    positions = jnp.arange(2 * TOK_DEV, dtype=jnp.int32)
    inside = (positions[None, :, None] >= starts[:, None, :]) & (positions[None, :, None] < ends[:, None, :])
    has_pos = jnp.any(inside, axis=2)
    label_pos = jnp.sum(inside.astype(jnp.int32) * labels[None, None, :], axis=2)
    order_keys = jax.random.split(key_order, blocks)
    ranks = jax.vmap(lambda single: jax.random.permutation(single, TOK_DEV))(order_keys)
    first_has = jnp.take_along_axis(has_pos[:, :TOK_DEV], ranks, axis=1)
    first_label = jnp.take_along_axis(label_pos[:, :TOK_DEV], ranks, axis=1)
    second_has = jnp.take_along_axis(has_pos[:, TOK_DEV:], ranks, axis=1)
    second_label = jnp.take_along_axis(label_pos[:, TOK_DEV:], ranks, axis=1)
    others = EXPERTS - WINDOW
    scores = jax.random.randint(key_score, (blocks, TOK_DEV, others), 0, 1 << 20) * EXPERTS
    scores = scores + jnp.arange(others, dtype=jnp.int32)[None, None, :]
    unused, picks = lax.top_k(scores, TOPK)
    picks = picks.astype(jnp.int32) + WINDOW
    slot_one = jax.random.randint(key_slot, (blocks, TOK_DEV), 0, TOPK)
    slot_two = (slot_one + jax.random.randint(key_step, (blocks, TOK_DEV), 1, TOPK)) % TOPK
    places = jnp.arange(TOPK, dtype=jnp.int32)
    use_one = first_has[:, :, None] & (places[None, None, :] == slot_one[:, :, None])
    use_two = second_has[:, :, None] & (places[None, None, :] == slot_two[:, :, None])
    routes = jnp.where(use_one, first_label[:, :, None], picks)
    routes = jnp.where(use_two, second_label[:, :, None], routes)
    return routes.reshape(TOKENS, TOPK).astype(jnp.int32)


def spiked(result, own_key, source, target, parts, factor):
    owner, partner = [(jnp.arange(result.shape[position]) // (result.shape[position] // parts)).reshape([-1 if axis == position else 1 for axis in range(result.ndim)]) for position in (source, target)]
    chosen = jax.random.permutation(own_key, parts)[partner]
    strong = (owner == chosen) | (owner == (partner + parts // 2) % parts)
    return jnp.where(strong, factor * result, result)


def block_scale(own_key, shape, pieces, low, high):
    gain, own = 1.0, jax.random.fold_in(own_key, 6)
    for position, parts in pieces:
        draws = jnp.exp(jax.random.uniform(jax.random.fold_in(own, position), (parts,), jnp.float32, low / len(pieces), high / len(pieces)))
        gain = gain * jnp.repeat(draws, shape[position] // parts).reshape([-1 if axis == position else 1 for axis in range(len(shape))])
    return gain


def noise(key, shape, deviation, limit, pieces=(), held_as=jnp.bfloat16):
    result = jax.random.normal(key, shape, jnp.float32) * deviation
    if len(pieces) > 0:
        result = block_scale(key, shape, pieces, -0.22, 0.18) * result
    return jnp.clip(result, min=-limit, max=limit).astype(held_as)


def noise_with(own_key, extent, spread, most, shards, heavy, kind=jnp.bfloat16):
    values = spread * jax.random.normal(own_key, extent, jnp.float32)
    if shards:
        values = values * block_scale(own_key, extent, shards, -0.22, 0.18)
    return jnp.clip(spiked(values, jax.random.fold_in(own_key, 3), *heavy), -most, most).astype(kind)


def setup_inputs(seed: int = 0) -> dict:
    streams_of = jax.random.split(jax.random.key(seed), 8)
    inputs = noise(streams_of[0], (TOKENS, D), 1.0, 6.0, ((0, 32),))
    out_grad = noise_with(streams_of[1], (TOKENS, D), 1.0, 6.0, ((0, 32),), (0, 1, 32, 2.75))
    routes = draw_routes(jax.random.fold_in(streams_of[7], 71), 0)
    gate_probs = jnp.clip(jnp.exp(math.log(0.6) - 2.4849067 * jax.random.uniform(streams_of[3], (TOKENS, TOPK), jnp.float32) ** block_scale(streams_of[3], (TOKENS, TOPK), ((0, 32),), -0.2, 0.2)), 0.05, 0.6)
    gate_weight = noise(streams_of[4], (WINDOW, D, F), D ** -0.5, 0.125, ((0, 4),))
    up_weight = noise(streams_of[5], (WINDOW, D, F), D ** -0.5, 0.125, ((0, 4),))
    down_weight = noise(streams_of[6], (WINDOW, F, D), F ** -0.5, 0.21875, ((0, 4),))
    return dict(inputs=inputs, out_grad=out_grad, routes=routes, gate_probs=gate_probs, gate_weight=gate_weight, up_weight=up_weight, down_weight=down_weight)


coef_linear = 3.4445
coef_cubic = -4.775
coef_quintic = 2.0315
norm_eps = 1e-06
highest = lax.Precision.HIGHEST
rows_first = (((0,), (0,)), ((), ()))
cols_last = (((1,), (1,)), ((), ()))

def newton_schulz(summed):
    total = jnp.sum(summed * summed)
    current = summed / (jnp.sqrt(total) + norm_eps)
    for step in range(ITERS):
        gram = lax.dot_general(current, current, rows_first, precision=highest, preferred_element_type=jnp.float32)
        square = jnp.dot(gram, gram, precision=highest, preferred_element_type=jnp.float32)
        poly = coef_cubic * gram + coef_quintic * square
        current = coef_linear * current + jnp.dot(current, poly, precision=highest, preferred_element_type=jnp.float32)
    return current

def reference(inputs, out_grad, routes, gate_probs, gate_weight, up_weight, down_weight):
    rows_most = GROUPS * WINDOW * CAP

    def one_expert(carry, item):
        index, w_gate, w_up, w_down = item
        named = routes == index
        weight = lax.optimization_barrier(jnp.sum(jnp.where(named, gate_probs, jnp.float32(0.0)), axis=1))
        chosen = jnp.any(named, axis=1)
        picked = jnp.nonzero(chosen, size=rows_most, fill_value=0)[0].astype(jnp.int32)
        live = jnp.arange(rows_most) < jnp.sum(chosen.astype(jnp.int32))
        rows_in = jnp.where(live[:, None], inputs[picked], jnp.zeros((), inputs.dtype))
        scaled = (out_grad[picked].astype(jnp.float32) * weight[picked][:, None]).astype(jnp.bfloat16)
        scaled = jnp.where(live[:, None], scaled, jnp.zeros((), scaled.dtype))
        pre_gate = jnp.dot(rows_in, w_gate, preferred_element_type=jnp.float32)
        pre_up = jnp.dot(rows_in, w_up, preferred_element_type=jnp.float32)
        sigma = jax.nn.sigmoid(pre_gate)
        swish = pre_gate * sigma
        hidden = (swish * pre_up).astype(jnp.bfloat16)
        d_hidden = lax.dot_general(scaled, w_down, cols_last, preferred_element_type=jnp.float32)
        d_up = (d_hidden * swish).astype(jnp.bfloat16)
        d_gate = (d_hidden * pre_up * sigma * (1.0 + pre_gate * (1.0 - sigma))).astype(jnp.bfloat16)
        back = lax.dot_general(d_gate, w_gate, cols_last, preferred_element_type=jnp.float32)
        back = back + lax.dot_general(d_up, w_up, cols_last, preferred_element_type=jnp.float32)
        back = back.astype(jnp.bfloat16).astype(jnp.float32)
        carry = carry.at[picked].add(jnp.where(live[:, None], back, jnp.float32(0.0)))
        gate_sum = lax.dot_general(rows_in, d_gate, rows_first, preferred_element_type=jnp.float32) / GROUPS
        up_sum = lax.dot_general(rows_in, d_up, rows_first, preferred_element_type=jnp.float32) / GROUPS
        down_sum = lax.dot_general(scaled, hidden, rows_first, preferred_element_type=jnp.float32) / GROUPS
        return (carry, (gate_sum, up_sum, newton_schulz(down_sum)))
    indices = jnp.arange(WINDOW).astype(jnp.int32)
    start = jnp.zeros(inputs.shape, jnp.float32)
    total, outputs = lax.scan(one_expert, start, (indices, gate_weight, up_weight, down_weight))
    gate_grad, up_grad, down_update = outputs
    return (total.astype(jnp.bfloat16), gate_grad, up_grad, down_update)
```

```python
import jax
import jax.numpy as jnp
from jax import lax
from jax.sharding import PartitionSpec as P

ITERS = 3
CAP = 16


coef_linear = 3.4445
coef_cubic = -4.775
coef_quintic = 2.0315
norm_eps = 1e-06
rows_first = (((0,), (0,)), ((), ()))
cols_last = (((1,), (1,)), ((), ()))


def slot_tables(routes, gate_probs, owners, capacity):
    count, picks = routes.shape
    flat = routes.reshape(count * picks)
    labels = jnp.arange(owners, dtype=jnp.int32)
    onehot = (flat[:, None] == labels[None, :]).astype(jnp.int32)
    before = jnp.cumsum(onehot, axis=0) - onehot
    place = jnp.sum(before * onehot, axis=1)
    target = jnp.where(flat < owners, flat * capacity + place, -1)
    slots = jnp.arange(owners * capacity, dtype=jnp.int32)
    match = (target[None, :] == slots[:, None]).reshape(owners * capacity, count, picks)
    dispatch = jnp.sum(match.astype(jnp.float32), axis=2).astype(jnp.bfloat16)
    weight = jnp.sum(jnp.where(match, gate_probs[None, :, :], jnp.float32(0.0)), axis=(1, 2))
    return (dispatch, weight)


high = lax.Precision.HIGH


def mul(left, right):
    return jnp.dot(left, right, precision=high, preferred_element_type=jnp.float32)


def factor(power, identity):
    return coef_linear * identity + coef_cubic * power + coef_quintic * mul(power, power)


def small_rows(rows_own, rows_all, hidden, groups):
    outer = lax.dot_general(rows_all, rows_all, cols_last, preferred_element_type=jnp.float32)
    hid = lax.dot_general(hidden, hidden, cols_last, preferred_element_type=jnp.float32)
    total = jnp.maximum(jnp.sum(outer * hid), 0.0) / (groups * groups)
    scale = 1.0 / (groups * (jnp.sqrt(total) + norm_eps))
    power = mul(hid * scale, outer * scale)
    identity = jnp.eye(power.shape[0], dtype=jnp.float32)
    left = rows_own.astype(jnp.float32).T * scale
    for step in range(ITERS):
        step_factor = factor(power, identity)
        left = mul(left, step_factor)
        if step < ITERS - 1:
            power = mul(mul(power, step_factor), step_factor)
    return mul(left, hidden.astype(jnp.float32))


def small_units(rows_own, rows_all, hidden, groups):
    whole = lax.dot_general(rows_all, hidden, rows_first, preferred_element_type=jnp.float32) / groups
    own = lax.dot_general(rows_own, hidden, rows_first, preferred_element_type=jnp.float32) / groups
    norm = jnp.sqrt(jnp.sum(whole * whole)) + norm_eps
    whole = whole / norm
    own = own / norm
    power = lax.dot_general(
        whole, whole, rows_first, precision=high, preferred_element_type=jnp.float32
    )
    identity = jnp.eye(power.shape[0], dtype=jnp.float32)
    for step in range(ITERS):
        step_factor = factor(power, identity)
        own = mul(own, step_factor)
        if step < ITERS - 1:
            power = mul(mul(power, step_factor), step_factor)
    return own


def per_device(inputs, out_grad, routes, gate_probs, gate_weight, up_weight, down_weight):
    owners = lax.axis_size("ep")
    groups = lax.axis_size("rep")
    width = inputs.shape[1]
    dispatch, weight = slot_tables(routes, gate_probs, owners, CAP)
    rows_send = jnp.dot(dispatch, inputs, preferred_element_type=jnp.float32).astype(jnp.bfloat16)
    grad_send = jnp.dot(dispatch, out_grad, preferred_element_type=jnp.float32) * weight[:, None]
    grad_send = grad_send.astype(jnp.bfloat16)
    rows = owners * CAP
    both_send = jnp.concatenate([rows_send, grad_send], axis=1)
    both_recv = lax.all_to_all(
        both_send.reshape(owners, CAP, 2 * width), "ep", split_axis=0, concat_axis=0, tiled=True
    ).reshape(rows, 2 * width)
    rows_recv = both_recv[:, :width]
    scaled = both_recv[:, width:]
    scaled_all = lax.all_gather(scaled, "rep", axis=0, tiled=True)
    rows_own = lax.all_to_all(
        rows_recv.reshape(rows, groups, width // groups).transpose(1, 0, 2),
        "rep", split_axis=0, concat_axis=0, tiled=True,
    ).reshape(groups * rows, width // groups)
    w_gate = gate_weight[0]
    w_up = up_weight[0]
    w_down = down_weight[0]
    units = w_gate.shape[1]
    pre_gate = jnp.dot(rows_recv, w_gate, preferred_element_type=jnp.float32)
    pre_up = jnp.dot(rows_recv, w_up, preferred_element_type=jnp.float32)
    sigma = jax.nn.sigmoid(pre_gate)
    swish = pre_gate * sigma
    hidden = (swish * pre_up).astype(jnp.bfloat16)
    d_hidden = lax.dot_general(scaled, w_down, cols_last, preferred_element_type=jnp.float32)
    d_up = (d_hidden * swish).astype(jnp.bfloat16)
    d_gate = (d_hidden * pre_up * sigma * (1.0 + pre_gate * (1.0 - sigma))).astype(jnp.bfloat16)
    back = lax.dot_general(d_gate, w_gate, cols_last, preferred_element_type=jnp.float32)
    back = (
        back + lax.dot_general(d_up, w_up, cols_last, preferred_element_type=jnp.float32)
    ).astype(jnp.bfloat16)
    returned = lax.all_to_all(
        back.reshape(owners, CAP, width), "ep", split_axis=0, concat_axis=0, tiled=True
    ).reshape(owners * CAP, width)
    input_grad = lax.dot_general(
        dispatch, returned, rows_first, preferred_element_type=jnp.float32
    ).astype(jnp.bfloat16)
    units_all = lax.all_gather(
        jnp.concatenate([d_gate, d_up, hidden], axis=1), "rep", axis=0, tiled=True
    )
    both = lax.dot_general(
        rows_own, units_all[:, : 2 * units], rows_first, preferred_element_type=jnp.float32
    ) / groups
    gate_grad = both[:, :units]
    up_grad = both[:, units:]
    hidden_all = units_all[:, 2 * units :]
    share = width // groups
    scaled_own = lax.dynamic_slice_in_dim(scaled_all, lax.axis_index("rep") * share, share, axis=1)
    form = small_rows if groups * rows < units else small_units
    down_update = form(scaled_own, scaled_all, hidden_all, groups)
    return (input_grad, gate_grad[None], up_grad[None], down_update[None])


def solution(mesh):
    in_specs = (
        P(("rep", "ep"), None),
        P(("rep", "ep"), None),
        P(("rep", "ep"), None),
        P(("rep", "ep"), None),
        P("ep", None, None),
        P("ep", None, None),
        P("ep", None, None),
    )
    out_specs = (
        P(("rep", "ep"), None),
        P("ep", "rep", None),
        P("ep", "rep", None),
        P("ep", "rep", None),
    )
    return jax.shard_map(
        per_device, mesh=mesh, in_specs=in_specs, out_specs=out_specs, check_vma=False
    )
```

```python
import functools

import jax
import jax.numpy as jnp
from jax import lax
from jax.experimental import pallas as pl
from jax.experimental.pallas import tpu as pltpu
from jax.sharding import PartitionSpec as P

ITERS = 3
CAP = 16


coef_linear = 3.4445
coef_cubic = -4.775
coef_quintic = 2.0315
norm_eps = 1e-06
rows_first = (((0,), (0,)), ((), ()))
cols_last = (((1,), (1,)), ((), ()))


def slot_tables(routes, gate_probs, owners, capacity):
    count, picks = routes.shape
    flat = routes.reshape(count * picks)
    labels = jnp.arange(owners, dtype=jnp.int32)
    onehot = (flat[:, None] == labels[None, :]).astype(jnp.int32)
    before = jnp.cumsum(onehot, axis=0) - onehot
    place = jnp.sum(before * onehot, axis=1)
    target = jnp.where(flat < owners, flat * capacity + place, -1)
    slots = jnp.arange(owners * capacity, dtype=jnp.int32)
    match = (target[None, :] == slots[:, None]).reshape(owners * capacity, count, picks)
    dispatch = jnp.sum(match.astype(jnp.float32), axis=2).astype(jnp.bfloat16)
    weight = jnp.sum(jnp.where(match, gate_probs[None, :, :], jnp.float32(0.0)), axis=(1, 2))
    return (dispatch, weight)


high = lax.Precision.HIGH


def mul(left, right):
    return jnp.dot(left, right, precision=high, preferred_element_type=jnp.float32)


def factor(power, identity):
    return coef_linear * identity + coef_cubic * power + coef_quintic * mul(power, power)


def small_rows(rows_own, rows_all, hidden, groups):
    outer = lax.dot_general(rows_all, rows_all, cols_last, preferred_element_type=jnp.float32)
    hid = lax.dot_general(hidden, hidden, cols_last, preferred_element_type=jnp.float32)
    total = jnp.maximum(jnp.sum(outer * hid), 0.0) / (groups * groups)
    scale = 1.0 / (groups * (jnp.sqrt(total) + norm_eps))
    power = mul(hid * scale, outer * scale)
    identity = jnp.eye(power.shape[0], dtype=jnp.float32)
    left = rows_own.astype(jnp.float32).T * scale
    for step in range(ITERS):
        step_factor = factor(power, identity)
        left = mul(left, step_factor)
        if step < ITERS - 1:
            power = mul(mul(power, step_factor), step_factor)
    return mul(left, hidden.astype(jnp.float32))


def small_units(rows_own, rows_all, hidden, groups):
    whole = lax.dot_general(rows_all, hidden, rows_first, preferred_element_type=jnp.float32) / groups
    own = lax.dot_general(rows_own, hidden, rows_first, preferred_element_type=jnp.float32) / groups
    norm = jnp.sqrt(jnp.sum(whole * whole)) + norm_eps
    whole = whole / norm
    own = own / norm
    power = lax.dot_general(
        whole, whole, rows_first, precision=high, preferred_element_type=jnp.float32
    )
    identity = jnp.eye(power.shape[0], dtype=jnp.float32)
    for step in range(ITERS):
        step_factor = factor(power, identity)
        own = mul(own, step_factor)
        if step < ITERS - 1:
            power = mul(mul(power, step_factor), step_factor)
    return own


rows_cols = (((1,), (0,)), ((), ()))


def dot(left, right, dims=rows_cols):
    return lax.dot_general(left, right, dims, preferred_element_type=jnp.float32)


def split(value):
    top = value.astype(jnp.bfloat16)
    return top, (value - top.astype(jnp.float32)).astype(jnp.bfloat16)


def dot3(left, right):
    return dot(left[0], right[0]) + (dot(left[0], right[1]) + dot(left[1], right[0]))


def remote(src, dst, send, recv, device):
    return pltpu.make_async_remote_copy(
        src_ref=src, dst_ref=dst, send_sem=send, recv_sem=recv,
        device_id=device, device_id_type=pl.DeviceIdType.MESH,
    )


def kernel(
    owners, groups,
    inputs, out_grad, routes, gate_probs, gate_hbm, up_hbm, down_hbm,
    input_grad, gate_grad, up_grad, down_update,
    w_gate, w_up, w_down, x_send, g_send, x_recv, s_all, h_all, d_all, x_own, back_send, ret,
    w_sem, xs_sem, xr_sem, gs_sem, gr_sem, bs_sem, br_sem,
    os_sem, or_sem, ss_sem, sr_sem, hs_sem, hr_sem, ds_sem, dr_sem,
):
    me = lax.axis_index("ep")
    rep = lax.axis_index("rep")
    core = rep % 2
    chip = rep // 2
    chips = groups // 2
    sibling = chip * 2 + (1 - core)
    tokens, width = inputs.shape
    units = h_all.shape[2]
    rows = owners * CAP
    share = width // groups
    near = [(me + k) % owners for k in range(1, owners)]
    far = [((chip + k) % chips) * 2 + core for k in range(1, chips)]
    others = [(rep + k) % groups for k in range(1, groups)]

    loads = [
        pltpu.make_async_copy(src, dst, w_sem.at[n])
        for n, (src, dst) in enumerate(((gate_hbm.at[0], w_gate), (up_hbm.at[0], w_up), (down_hbm.at[0], w_down)))
    ]
    for load in loads:
        load.start()
    barrier = pltpu.get_barrier_semaphore()
    for peer in near:
        pl.semaphore_signal(barrier, inc=1, device_id={"ep": peer}, device_id_type=pl.DeviceIdType.MESH)
    for peer in others:
        pl.semaphore_signal(barrier, inc=1, device_id={"rep": peer}, device_id_type=pl.DeviceIdType.MESH)

    lane = lax.broadcasted_iota(jnp.int32, (tokens, 128), 1)
    place = (lane % CAP).astype(jnp.float32)
    expert = jnp.where(lane < rows, lane // CAP, -1)
    named = jnp.zeros((tokens, 128), jnp.float32)
    weight = jnp.zeros((tokens, 128), jnp.float32)
    for k in range(routes.shape[1]):
        hit = routes[:, k : k + 1] == expert
        named = named + jnp.where(hit, 1.0, 0.0)
        weight = weight + jnp.where(hit, gate_probs[:, k : k + 1], 0.0)
    earlier = lax.broadcasted_iota(jnp.int32, (tokens, tokens), 1) < lax.broadcasted_iota(
        jnp.int32, (tokens, tokens), 0
    )
    before = dot(jnp.where(earlier, 1.0, 0.0).astype(jnp.bfloat16), named.astype(jnp.bfloat16))
    slots = jnp.where(before == place, named, 0.0)
    dispatch = slots.T[:rows].astype(jnp.bfloat16)
    weight = jnp.sum((slots * weight).T[:rows], axis=1, keepdims=True)
    x_send[...] = dot(dispatch, inputs[...]).astype(jnp.bfloat16).reshape(owners, CAP, width)
    pl.semaphore_wait(barrier, len(near) + len(others))
    sends = []

    def send(*spec):
        copy = remote(*spec)
        copy.start()
        sends.append(copy)

    for n, peer in enumerate(near):
        send(x_send.at[peer], x_recv.at[me], xs_sem.at[n], xr_sem.at[me], {"ep": peer})
    g_send[...] = (dot(dispatch, out_grad[...]) * weight).astype(jnp.bfloat16).reshape(owners, CAP, width)
    for n, peer in enumerate(near):
        send(g_send.at[peer], s_all.at[rep, me], gs_sem.at[n], gr_sem.at[me], {"ep": peer})
    x_recv[me] = x_send[me]
    s_all[rep, me] = g_send[me]

    def arrived(ref, recv, peer):
        remote(ref, ref, xs_sem.at[0], recv, {"ep": peer}).wait_recv()

    def spread(ref, send_sem, recv_sem):
        for n, peer in enumerate(far):
            send(ref.at[rep], ref.at[rep], send_sem.at[n], recv_sem.at[rep], {"rep": peer})
        send(ref.at[rep], ref.at[rep], send_sem.at[len(far)], recv_sem.at[rep], {"rep": sibling})

    def swap(ref, send_sem, recv_sem):
        for n, peer in enumerate(far):
            arrived(ref.at[peer], recv_sem.at[peer], near[0])
            send(ref.at[peer], ref.at[peer], send_sem.at[chips + n], recv_sem.at[peer], {"rep": sibling})

    def finish(ref, recv_sem):
        for k in range(chips):
            source = ((chip + k) % chips) * 2 + (1 - core)
            arrived(ref.at[source], recv_sem.at[source], near[0])

    loads[0].wait()
    loads[1].wait()
    for peer in near:
        arrived(x_recv.at[peer], xr_sem.at[peer], peer)
    x = x_recv[...].reshape(rows, width)
    pre_gate = dot(x, w_gate[...])
    pre_up = dot(x, w_up[...])
    sigma = jax.nn.sigmoid(pre_gate)
    swish = pre_gate * sigma
    h_all[rep] = (swish * pre_up).astype(jnp.bfloat16)
    spread(h_all, hs_sem, hr_sem)
    loads[2].wait()
    for peer in near:
        arrived(s_all.at[rep, peer], gr_sem.at[peer], peer)
    spread(s_all, ss_sem, sr_sem)
    d_hidden = dot(s_all[rep].reshape(rows, width), w_down[...], cols_last)
    d_up = (d_hidden * swish).astype(jnp.bfloat16)
    d_gate = (d_hidden * pre_up * sigma * (1.0 + pre_gate * (1.0 - sigma))).astype(jnp.bfloat16)
    d_all[rep, :, :units] = d_gate
    d_all[rep, :, units:] = d_up
    spread(d_all, ds_sem, dr_sem)
    for n, peer in enumerate(others):
        columns = pl.ds(pl.multiple_of(peer * share, 128), share)
        send(x_recv.at[:, :, columns], x_own.at[rep], os_sem.at[n], or_sem.at[rep], {"rep": peer})
    mine = pl.ds(pl.multiple_of(rep * share, 128), share)
    x_own[rep] = x_recv[:, :, mine]
    swap(h_all, hs_sem, hr_sem)
    back = dot(d_gate, w_gate[...], cols_last) + dot(d_up, w_up[...], cols_last)
    back_send[...] = back.astype(jnp.bfloat16).reshape(owners, CAP, width)
    for n, peer in enumerate(near):
        send(back_send.at[peer], ret.at[me], bs_sem.at[n], br_sem.at[me], {"ep": peer})
    ret[me] = back_send[me]
    finish(h_all, hr_sem)
    hidden = h_all[...].reshape(groups * rows, units)
    hid = dot(hidden, hidden, cols_last)
    swap(s_all, ss_sem, sr_sem)
    finish(s_all, sr_sem)
    scaled = s_all[...].reshape(groups * rows, width)
    outer = dot(scaled, scaled, cols_last)
    total = jnp.sum(jnp.sum(outer * hid, axis=0, keepdims=True), axis=1, keepdims=True)
    total = jnp.maximum(total, 0.0) / (groups * groups)
    scale = 1.0 / (groups * (jnp.sqrt(total) + norm_eps))
    power = dot3(split(outer * scale), split(hid * scale))
    left = s_all[:, :, :, mine].reshape(groups * rows, share).astype(jnp.float32) * scale
    swap(d_all, ds_sem, dr_sem)
    size = groups * rows
    diagonal = lax.broadcasted_iota(jnp.int32, (size, size), 0) == lax.broadcasted_iota(
        jnp.int32, (size, size), 1
    )
    for step in range(ITERS):
        parts = split(power)
        poly = coef_cubic * power + coef_quintic * dot3(parts, parts)
        poly = split(poly + jnp.where(diagonal, coef_linear, 0.0))
        left = dot3(poly, split(left))
        if step < ITERS - 1:
            power = dot3(split(dot3(parts, poly)), poly)
    left = split(left)
    down_update[0] = dot(left[0], hidden, rows_first) + dot(left[1], hidden, rows_first)
    for peer in near:
        arrived(ret.at[peer], br_sem.at[peer], peer)
    input_grad[...] = dot(
        slots[:, :rows].astype(jnp.bfloat16), ret[...].reshape(rows, width)
    ).astype(jnp.bfloat16)
    finish(d_all, dr_sem)
    for peer in others:
        arrived(x_own.at[peer], or_sem.at[peer], near[0])
    x_rows = x_own[...].reshape(groups * rows, share)
    both = dot(x_rows, d_all[...].reshape(groups * rows, 2 * units), rows_first) / groups
    gate_grad[0] = both[:, :units]
    up_grad[0] = both[:, units:]
    for copy in sends:
        copy.wait_send()


def fused(inputs, out_grad, routes, gate_probs, gate_weight, up_weight, down_weight):
    owners = lax.axis_size("ep")
    groups = lax.axis_size("rep")
    tokens, width = inputs.shape
    units = gate_weight.shape[2]
    rows = owners * CAP
    share = width // groups
    chips = groups // 2
    half = jnp.bfloat16
    inside = pl.BlockSpec(memory_space=pltpu.VMEM)
    outside = pl.BlockSpec(memory_space=pl.ANY)
    dma = pltpu.SemaphoreType.DMA
    grads = jax.ShapeDtypeStruct((1, share, units), jnp.float32)
    return pl.pallas_call(
        functools.partial(kernel, owners, groups),
        out_shape=(jax.ShapeDtypeStruct((tokens, width), half), grads, grads, grads),
        in_specs=[inside] * 4 + [outside] * 3,
        out_specs=(inside,) * 4,
        scratch_shapes=[
            pltpu.VMEM((width, units), half),
            pltpu.VMEM((width, units), half),
            pltpu.VMEM((units, width), half),
            pltpu.VMEM((owners, CAP, width), half),
            pltpu.VMEM((owners, CAP, width), half),
            pltpu.VMEM((owners, CAP, width), half),
            pltpu.VMEM((groups, owners, CAP, width), half),
            pltpu.VMEM((groups, rows, units), half),
            pltpu.VMEM((groups, rows, 2 * units), half),
            pltpu.VMEM((groups, owners, CAP, share), half),
            pltpu.VMEM((owners, CAP, width), half),
            pltpu.VMEM((owners, CAP, width), half),
            dma((3,)),
        ]
        + [dma((owners,))] * 6
        + [dma((groups,))] * 8,
        compiler_params=pltpu.CompilerParams(
            collective_id=0, has_side_effects=True, vmem_limit_bytes=52 * 1024 * 1024
        ),
    )(inputs, out_grad, routes, gate_probs, gate_weight, up_weight, down_weight)


def per_device(inputs, out_grad, routes, gate_probs, gate_weight, up_weight, down_weight):
    owners = lax.axis_size("ep")
    groups = lax.axis_size("rep")
    width = inputs.shape[1]
    rows = owners * CAP
    if groups * rows < gate_weight.shape[2] and rows <= 128 and groups % 2 == 0:
        return fused(inputs, out_grad, routes, gate_probs, gate_weight, up_weight, down_weight)
    dispatch, weight = slot_tables(routes, gate_probs, owners, CAP)
    rows_send = jnp.dot(dispatch, inputs, preferred_element_type=jnp.float32).astype(jnp.bfloat16)
    grad_send = jnp.dot(dispatch, out_grad, preferred_element_type=jnp.float32) * weight[:, None]
    grad_send = grad_send.astype(jnp.bfloat16)
    both_send = jnp.concatenate([rows_send, grad_send], axis=1)
    both_recv = lax.all_to_all(
        both_send.reshape(owners, CAP, 2 * width), "ep", split_axis=0, concat_axis=0, tiled=True
    ).reshape(rows, 2 * width)
    rows_recv = both_recv[:, :width]
    scaled = both_recv[:, width:]
    scaled_all = lax.all_gather(scaled, "rep", axis=0, tiled=True)
    rows_own = lax.all_to_all(
        rows_recv.reshape(rows, groups, width // groups).transpose(1, 0, 2),
        "rep", split_axis=0, concat_axis=0, tiled=True,
    ).reshape(groups * rows, width // groups)
    w_gate = gate_weight[0]
    w_up = up_weight[0]
    w_down = down_weight[0]
    units = w_gate.shape[1]
    pre_gate = jnp.dot(rows_recv, w_gate, preferred_element_type=jnp.float32)
    pre_up = jnp.dot(rows_recv, w_up, preferred_element_type=jnp.float32)
    sigma = jax.nn.sigmoid(pre_gate)
    swish = pre_gate * sigma
    hidden = (swish * pre_up).astype(jnp.bfloat16)
    d_hidden = lax.dot_general(scaled, w_down, cols_last, preferred_element_type=jnp.float32)
    d_up = (d_hidden * swish).astype(jnp.bfloat16)
    d_gate = (d_hidden * pre_up * sigma * (1.0 + pre_gate * (1.0 - sigma))).astype(jnp.bfloat16)
    back = lax.dot_general(d_gate, w_gate, cols_last, preferred_element_type=jnp.float32)
    back = (
        back + lax.dot_general(d_up, w_up, cols_last, preferred_element_type=jnp.float32)
    ).astype(jnp.bfloat16)
    returned = lax.all_to_all(
        back.reshape(owners, CAP, width), "ep", split_axis=0, concat_axis=0, tiled=True
    ).reshape(owners * CAP, width)
    input_grad = lax.dot_general(
        dispatch, returned, rows_first, preferred_element_type=jnp.float32
    ).astype(jnp.bfloat16)
    units_all = lax.all_gather(
        jnp.concatenate([d_gate, d_up, hidden], axis=1), "rep", axis=0, tiled=True
    )
    both = lax.dot_general(
        rows_own, units_all[:, : 2 * units], rows_first, preferred_element_type=jnp.float32
    ) / groups
    gate_grad = both[:, :units]
    up_grad = both[:, units:]
    hidden_all = units_all[:, 2 * units :]
    share = width // groups
    scaled_own = lax.dynamic_slice_in_dim(scaled_all, lax.axis_index("rep") * share, share, axis=1)
    form = small_rows if groups * rows < units else small_units
    down_update = form(scaled_own, scaled_all, hidden_all, groups)
    return (input_grad, gate_grad[None], up_grad[None], down_update[None])


def solution(mesh):
    in_specs = (
        P(("rep", "ep"), None),
        P(("rep", "ep"), None),
        P(("rep", "ep"), None),
        P(("rep", "ep"), None),
        P("ep", None, None),
        P("ep", None, None),
        P("ep", None, None),
    )
    out_specs = (
        P(("rep", "ep"), None),
        P("ep", "rep", None),
        P("ep", "rep", None),
        P("ep", "rep", None),
    )
    return jax.shard_map(
        per_device, mesh=mesh, in_specs=in_specs, out_specs=out_specs, check_vma=False
    )
```

```python
import functools

import jax
import jax.numpy as jnp
from jax import lax
from jax.experimental import pallas as pl
from jax.experimental.pallas import tpu as pltpu
from jax.sharding import PartitionSpec as P

ITERS = 3
CAP = 16


coef_linear = 3.4445
coef_cubic = -4.775
coef_quintic = 2.0315
norm_eps = 1e-06
rows_first = (((0,), (0,)), ((), ()))
cols_last = (((1,), (1,)), ((), ()))


def slot_tables(routes, gate_probs, owners, capacity):
    count, picks = routes.shape
    flat = routes.reshape(count * picks)
    labels = jnp.arange(owners, dtype=jnp.int32)
    onehot = (flat[:, None] == labels[None, :]).astype(jnp.int32)
    before = jnp.cumsum(onehot, axis=0) - onehot
    place = jnp.sum(before * onehot, axis=1)
    target = jnp.where(flat < owners, flat * capacity + place, -1)
    slots = jnp.arange(owners * capacity, dtype=jnp.int32)
    match = (target[None, :] == slots[:, None]).reshape(owners * capacity, count, picks)
    dispatch = jnp.sum(match.astype(jnp.float32), axis=2).astype(jnp.bfloat16)
    weight = jnp.sum(jnp.where(match, gate_probs[None, :, :], jnp.float32(0.0)), axis=(1, 2))
    return (dispatch, weight)


high = lax.Precision.HIGH


def mul(left, right):
    return jnp.dot(left, right, precision=high, preferred_element_type=jnp.float32)


def factor(power, identity):
    return coef_linear * identity + coef_cubic * power + coef_quintic * mul(power, power)


def small_rows(rows_own, rows_all, hidden, groups):
    outer = lax.dot_general(rows_all, rows_all, cols_last, preferred_element_type=jnp.float32)
    hid = lax.dot_general(hidden, hidden, cols_last, preferred_element_type=jnp.float32)
    total = jnp.maximum(jnp.sum(outer * hid), 0.0) / (groups * groups)
    scale = 1.0 / (groups * (jnp.sqrt(total) + norm_eps))
    power = mul(hid * scale, outer * scale)
    identity = jnp.eye(power.shape[0], dtype=jnp.float32)
    left = rows_own.astype(jnp.float32).T * scale
    for step in range(ITERS):
        step_factor = factor(power, identity)
        left = mul(left, step_factor)
        if step < ITERS - 1:
            power = mul(mul(power, step_factor), step_factor)
    return mul(left, hidden.astype(jnp.float32))


def small_units(rows_own, rows_all, hidden, groups):
    whole = lax.dot_general(rows_all, hidden, rows_first, preferred_element_type=jnp.float32) / groups
    own = lax.dot_general(rows_own, hidden, rows_first, preferred_element_type=jnp.float32) / groups
    norm = jnp.sqrt(jnp.sum(whole * whole)) + norm_eps
    whole = whole / norm
    own = own / norm
    power = lax.dot_general(
        whole, whole, rows_first, precision=high, preferred_element_type=jnp.float32
    )
    identity = jnp.eye(power.shape[0], dtype=jnp.float32)
    for step in range(ITERS):
        step_factor = factor(power, identity)
        own = mul(own, step_factor)
        if step < ITERS - 1:
            power = mul(mul(power, step_factor), step_factor)
    return own


rows_cols = (((1,), (0,)), ((), ()))


def dot(left, right, dims=rows_cols):
    return lax.dot_general(left, right, dims, preferred_element_type=jnp.float32)


def split(value):
    top = value.astype(jnp.bfloat16)
    return top, (value - top.astype(jnp.float32)).astype(jnp.bfloat16)


def dot3(left, right):
    return dot(left[0], right[0]) + (dot(left[0], right[1]) + dot(left[1], right[0]))


def remote(src, dst, send, recv, device):
    return pltpu.make_async_remote_copy(
        src_ref=src, dst_ref=dst, send_sem=send, recv_sem=recv,
        device_id=device, device_id_type=pl.DeviceIdType.MESH,
    )


def kernel(
    owners, groups,
    inputs_hbm, grad_hbm, routes, gate_probs, gate_hbm, up_hbm, down_hbm,
    input_grad, gate_grad, up_grad, down_update,
    inputs, out_grad, w_gate, w_up, w_down, x_send, g_send, x_recv, s_all, h_all, d_all, x_own, back_send, ret,
    w_sem, xs_sem, xr_sem, gs_sem, gr_sem, bs_sem, br_sem,
    os_sem, or_sem, ss_sem, sr_sem, hs_sem, hr_sem, ds_sem, dr_sem,
):
    me = lax.axis_index("ep")
    rep = lax.axis_index("rep")
    core = rep % 2
    chip = rep // 2
    chips = groups // 2
    sibling = chip * 2 + (1 - core)
    tokens, width = inputs.shape
    units = h_all.shape[2]
    rows = owners * CAP
    share = width // groups
    if owners == 4:
        near = [me + 1 - 2 * (me % 2), (me + 2) % 4, 3 - me]
    else:
        near = [(me + k) % owners for k in range(1, owners)]
    far = [((chip + k) % chips) * 2 + core for k in range(1, chips)]
    others = [(rep + k) % groups for k in range(1, groups)]

    barrier = pltpu.get_barrier_semaphore()
    for peer in near:
        pl.semaphore_signal(barrier, inc=1, device_id={"ep": peer}, device_id_type=pl.DeviceIdType.MESH)
    for peer in others:
        pl.semaphore_signal(barrier, inc=1, device_id={"rep": peer}, device_id_type=pl.DeviceIdType.MESH)

    loads = [
        pltpu.make_async_copy(src, dst, w_sem.at[n])
        for n, (src, dst) in enumerate(((gate_hbm.at[0], w_gate), (up_hbm.at[0], w_up), (down_hbm.at[0], w_down),
        (inputs_hbm, inputs), (grad_hbm, out_grad)))
    ]
    for n in (3, 4, 0, 1, 2):
        loads[n].start()
    line = lax.broadcasted_iota(jnp.int32, (rows, tokens), 0)
    place = (line % CAP).astype(jnp.float32)
    expert = line // CAP
    named = jnp.zeros((rows, tokens), jnp.float32)
    weight = jnp.zeros((rows, tokens), jnp.float32)
    for k in range(routes.shape[0]):
        hit = routes[k : k + 1, :] == expert
        named = named + jnp.where(hit, 1.0, 0.0)
        weight = weight + jnp.where(hit, gate_probs[k : k + 1, :], 0.0)
    earlier = lax.broadcasted_iota(jnp.int32, (tokens, tokens), 0) < lax.broadcasted_iota(
        jnp.int32, (tokens, tokens), 1
    )
    before = dot(named.astype(jnp.bfloat16), jnp.where(earlier, 1.0, 0.0).astype(jnp.bfloat16))
    slots = jnp.where(before == place, named, 0.0)
    dispatch = slots.astype(jnp.bfloat16)
    weight = jnp.sum(slots * weight, axis=1, keepdims=True)
    loads[3].wait()
    x_send[...] = dot(dispatch, inputs[...]).astype(jnp.bfloat16).reshape(owners, CAP, width)
    pl.semaphore_wait(barrier, len(near) + len(others))
    sends = []

    def send(*spec):
        copy = remote(*spec)
        copy.start()
        sends.append(copy)

    for n, peer in enumerate(near):
        send(x_send.at[peer], x_recv.at[me], xs_sem.at[n], xr_sem.at[me], {"ep": peer})
    loads[4].wait()
    g_send[...] = (dot(dispatch, out_grad[...]) * weight).astype(jnp.bfloat16).reshape(owners, CAP, width)
    for n, peer in enumerate(near):
        send(g_send.at[peer], s_all.at[rep, me], gs_sem.at[n], gr_sem.at[me], {"ep": peer})
    x_recv[me] = x_send[me]
    s_all[rep, me] = g_send[me]

    def arrived(ref, recv, peer):
        remote(ref, ref, xs_sem.at[0], recv, {"ep": peer}).wait_recv()

    def piece(j):
        block = s_all.at[rep, j]
        for n, peer in enumerate(far):
            send(block, block, ss_sem.at[n, j], sr_sem.at[rep, j], {"rep": peer})
        send(block, block, ss_sem.at[len(far), j], sr_sem.at[rep, j], {"rep": sibling})

    piece(me)

    def spread(ref, send_sem, recv_sem):
        for n, peer in enumerate(far):
            send(ref.at[rep], ref.at[rep], send_sem.at[n], recv_sem.at[rep], {"rep": peer})
        send(ref.at[rep], ref.at[rep], send_sem.at[len(far)], recv_sem.at[rep], {"rep": sibling})

    def swap(ref, send_sem, recv_sem):
        for n, peer in enumerate(far):
            arrived(ref.at[peer], recv_sem.at[peer], near[0])
            send(ref.at[peer], ref.at[peer], send_sem.at[chips + n], recv_sem.at[peer], {"rep": sibling})

    def finish(ref, recv_sem):
        for k in range(chips):
            source = ((chip + k) % chips) * 2 + (1 - core)
            arrived(ref.at[source], recv_sem.at[source], near[0])

    for peer in near:
        arrived(x_recv.at[peer], xr_sem.at[peer], peer)
    for n, peer in enumerate(others):
        columns = pl.ds(pl.multiple_of(peer * share, 128), share)
        send(x_recv.at[:, :, columns], x_own.at[rep], os_sem.at[n], or_sem.at[rep], {"rep": peer})
    loads[0].wait()
    loads[1].wait()
    x = x_recv[...].reshape(rows, width)
    pre_gate = dot(x, w_gate[...])
    pre_up = dot(x, w_up[...])
    sigma = jax.nn.sigmoid(pre_gate)
    swish = pre_gate * sigma
    h_all[rep] = (swish * pre_up).astype(jnp.bfloat16)
    spread(h_all, hs_sem, hr_sem)
    loads[2].wait()
    for peer in near:
        arrived(s_all.at[rep, peer], gr_sem.at[peer], peer)
        piece(peer)
    d_hidden = dot(s_all[rep].reshape(rows, width), w_down[...], cols_last)
    d_up = (d_hidden * swish).astype(jnp.bfloat16)
    d_gate = (d_hidden * pre_up * sigma * (1.0 + pre_gate * (1.0 - sigma))).astype(jnp.bfloat16)
    d_all[rep, :, :units] = d_gate
    d_all[rep, :, units:] = d_up
    mine = pl.ds(pl.multiple_of(rep * share, 128), share)
    x_own[rep] = x_recv[:, :, mine]
    swap(h_all, hs_sem, hr_sem)
    back = dot(d_gate, w_gate[...], cols_last) + dot(d_up, w_up[...], cols_last)
    back_send[...] = back.astype(jnp.bfloat16).reshape(owners, CAP, width)
    for n, peer in enumerate(near):
        send(back_send.at[peer], ret.at[me], bs_sem.at[n], br_sem.at[me], {"ep": peer})
    ret[me] = back_send[me]
    finish(h_all, hr_sem)
    hidden = h_all[...].reshape(groups * rows, units)
    hid = dot(hidden, hidden, cols_last)
    for j in [me] + near:
        for n, peer in enumerate(far):
            block = s_all.at[peer, j]
            arrived(block, sr_sem.at[peer, j], near[0])
            send(block, block, ss_sem.at[chips + n, j], sr_sem.at[peer, j], {"rep": sibling})
    spread(d_all, ds_sem, dr_sem)
    for j in [me] + near:
        for k in range(chips):
            source = ((chip + k) % chips) * 2 + (1 - core)
            arrived(s_all.at[source, j], sr_sem.at[source, j], near[0])
    scaled = s_all[...].reshape(groups * rows, width)
    outer = dot(scaled, scaled, cols_last)
    total = jnp.sum(jnp.sum(outer * hid, axis=0, keepdims=True), axis=1, keepdims=True)
    total = jnp.maximum(total, 0.0) / (groups * groups)
    scale = 1.0 / (groups * (jnp.sqrt(total) + norm_eps))
    power = dot3(split(outer * scale), split(hid * scale))
    left = s_all[:, :, :, mine].reshape(groups * rows, share).astype(jnp.float32) * scale
    size = groups * rows
    diagonal = lax.broadcasted_iota(jnp.int32, (size, size), 0) == lax.broadcasted_iota(
        jnp.int32, (size, size), 1
    )
    for step in range(ITERS):
        parts = split(power)
        poly = coef_cubic * power + coef_quintic * dot3(parts, parts)
        poly = split(poly + jnp.where(diagonal, coef_linear, 0.0))
        left = dot3(poly, split(left))
        if step < ITERS - 1:
            power = dot3(split(dot3(parts, poly)), poly)
        if step == ITERS - 2:
            swap(d_all, ds_sem, dr_sem)
    left = split(left)
    down_update[0] = dot(left[0], hidden, rows_first) + dot(left[1], hidden, rows_first)
    for peer in near:
        arrived(ret.at[peer], br_sem.at[peer], peer)
    input_grad[...] = dot(
        dispatch, ret[...].reshape(rows, width), rows_first
    ).astype(jnp.bfloat16)
    finish(d_all, dr_sem)
    for peer in others:
        arrived(x_own.at[peer], or_sem.at[peer], near[0])
    x_rows = x_own[...].reshape(groups * rows, share)
    both = dot(x_rows, d_all[...].reshape(groups * rows, 2 * units), rows_first) / groups
    gate_grad[0] = both[:, :units]
    up_grad[0] = both[:, units:]
    for copy in sends:
        copy.wait_send()


def fused(inputs, out_grad, routes, gate_probs, gate_weight, up_weight, down_weight):
    owners = lax.axis_size("ep")
    groups = lax.axis_size("rep")
    tokens, width = inputs.shape
    units = gate_weight.shape[2]
    rows = owners * CAP
    share = width // groups
    chips = groups // 2
    half = jnp.bfloat16
    inside = pl.BlockSpec(memory_space=pltpu.VMEM)
    outside = pl.BlockSpec(memory_space=pl.ANY)
    dma = pltpu.SemaphoreType.DMA
    grads = jax.ShapeDtypeStruct((1, share, units), jnp.float32)
    return pl.pallas_call(
        functools.partial(kernel, owners, groups),
        out_shape=(jax.ShapeDtypeStruct((tokens, width), half), grads, grads, grads),
        in_specs=[outside] * 2 + [inside] * 2 + [outside] * 3,
        out_specs=(inside,) * 4,
        scratch_shapes=[
            pltpu.VMEM((tokens, width), half),
            pltpu.VMEM((tokens, width), half),
            pltpu.VMEM((width, units), half),
            pltpu.VMEM((width, units), half),
            pltpu.VMEM((units, width), half),
            pltpu.VMEM((owners, CAP, width), half),
            pltpu.VMEM((owners, CAP, width), half),
            pltpu.VMEM((owners, CAP, width), half),
            pltpu.VMEM((groups, owners, CAP, width), half),
            pltpu.VMEM((groups, rows, units), half),
            pltpu.VMEM((groups, rows, 2 * units), half),
            pltpu.VMEM((groups, owners, CAP, share), half),
            pltpu.VMEM((owners, CAP, width), half),
            pltpu.VMEM((owners, CAP, width), half),
            dma((5,)),
        ]
        + [dma((owners,))] * 6
        + [dma((groups,))] * 2
        + [dma((groups, owners))] * 2
        + [dma((groups,))] * 4,
        compiler_params=pltpu.CompilerParams(
            collective_id=0, has_side_effects=True, vmem_limit_bytes=52 * 1024 * 1024
        ),
    )(inputs, out_grad, routes.T, gate_probs.T, gate_weight, up_weight, down_weight)


def per_device(inputs, out_grad, routes, gate_probs, gate_weight, up_weight, down_weight):
    owners = lax.axis_size("ep")
    groups = lax.axis_size("rep")
    width = inputs.shape[1]
    rows = owners * CAP
    if groups * rows < gate_weight.shape[2] and rows <= 128 and groups % 2 == 0:
        return fused(inputs, out_grad, routes, gate_probs, gate_weight, up_weight, down_weight)
    dispatch, weight = slot_tables(routes, gate_probs, owners, CAP)
    rows_send = jnp.dot(dispatch, inputs, preferred_element_type=jnp.float32).astype(jnp.bfloat16)
    grad_send = jnp.dot(dispatch, out_grad, preferred_element_type=jnp.float32) * weight[:, None]
    grad_send = grad_send.astype(jnp.bfloat16)
    both_send = jnp.concatenate([rows_send, grad_send], axis=1)
    both_recv = lax.all_to_all(
        both_send.reshape(owners, CAP, 2 * width), "ep", split_axis=0, concat_axis=0, tiled=True
    ).reshape(rows, 2 * width)
    rows_recv = both_recv[:, :width]
    scaled = both_recv[:, width:]
    scaled_all = lax.all_gather(scaled, "rep", axis=0, tiled=True)
    rows_own = lax.all_to_all(
        rows_recv.reshape(rows, groups, width // groups).transpose(1, 0, 2),
        "rep", split_axis=0, concat_axis=0, tiled=True,
    ).reshape(groups * rows, width // groups)
    w_gate = gate_weight[0]
    w_up = up_weight[0]
    w_down = down_weight[0]
    units = w_gate.shape[1]
    pre_gate = jnp.dot(rows_recv, w_gate, preferred_element_type=jnp.float32)
    pre_up = jnp.dot(rows_recv, w_up, preferred_element_type=jnp.float32)
    sigma = jax.nn.sigmoid(pre_gate)
    swish = pre_gate * sigma
    hidden = (swish * pre_up).astype(jnp.bfloat16)
    d_hidden = lax.dot_general(scaled, w_down, cols_last, preferred_element_type=jnp.float32)
    d_up = (d_hidden * swish).astype(jnp.bfloat16)
    d_gate = (d_hidden * pre_up * sigma * (1.0 + pre_gate * (1.0 - sigma))).astype(jnp.bfloat16)
    back = lax.dot_general(d_gate, w_gate, cols_last, preferred_element_type=jnp.float32)
    back = (
        back + lax.dot_general(d_up, w_up, cols_last, preferred_element_type=jnp.float32)
    ).astype(jnp.bfloat16)
    returned = lax.all_to_all(
        back.reshape(owners, CAP, width), "ep", split_axis=0, concat_axis=0, tiled=True
    ).reshape(owners * CAP, width)
    input_grad = lax.dot_general(
        dispatch, returned, rows_first, preferred_element_type=jnp.float32
    ).astype(jnp.bfloat16)
    units_all = lax.all_gather(
        jnp.concatenate([d_gate, d_up, hidden], axis=1), "rep", axis=0, tiled=True
    )
    both = lax.dot_general(
        rows_own, units_all[:, : 2 * units], rows_first, preferred_element_type=jnp.float32
    ) / groups
    gate_grad = both[:, :units]
    up_grad = both[:, units:]
    hidden_all = units_all[:, 2 * units :]
    share = width // groups
    scaled_own = lax.dynamic_slice_in_dim(scaled_all, lax.axis_index("rep") * share, share, axis=1)
    form = small_rows if groups * rows < units else small_units
    down_update = form(scaled_own, scaled_all, hidden_all, groups)
    return (input_grad, gate_grad[None], up_grad[None], down_update[None])


def solution(mesh):
    in_specs = (
        P(("rep", "ep"), None),
        P(("rep", "ep"), None),
        P(("rep", "ep"), None),
        P(("rep", "ep"), None),
        P("ep", None, None),
        P("ep", None, None),
        P("ep", None, None),
    )
    out_specs = (
        P(("rep", "ep"), None),
        P("ep", "rep", None),
        P("ep", "rep", None),
        P("ep", "rep", None),
    )
    return jax.shard_map(
        per_device, mesh=mesh, in_specs=in_specs, out_specs=out_specs, check_vma=False
    )
```

```python
import functools

import jax
import jax.numpy as jnp
from jax import lax
from jax.experimental import pallas as pl
from jax.experimental.pallas import tpu as pltpu
from jax.sharding import PartitionSpec as P

ITERS = 3
CAP = 16


coef_linear = 3.4445
coef_cubic = -4.775
coef_quintic = 2.0315
norm_eps = 1e-06
rows_first = (((0,), (0,)), ((), ()))
cols_last = (((1,), (1,)), ((), ()))


def slot_tables(routes, gate_probs, owners, capacity):
    count, picks = routes.shape
    flat = routes.reshape(count * picks)
    labels = jnp.arange(owners, dtype=jnp.int32)
    onehot = (flat[:, None] == labels[None, :]).astype(jnp.int32)
    before = jnp.cumsum(onehot, axis=0) - onehot
    place = jnp.sum(before * onehot, axis=1)
    target = jnp.where(flat < owners, flat * capacity + place, -1)
    slots = jnp.arange(owners * capacity, dtype=jnp.int32)
    match = (target[None, :] == slots[:, None]).reshape(owners * capacity, count, picks)
    dispatch = jnp.sum(match.astype(jnp.float32), axis=2).astype(jnp.bfloat16)
    weight = jnp.sum(jnp.where(match, gate_probs[None, :, :], jnp.float32(0.0)), axis=(1, 2))
    return (dispatch, weight)


high = lax.Precision.HIGH


def mul(left, right):
    return jnp.dot(left, right, precision=high, preferred_element_type=jnp.float32)


def factor(power, identity):
    return coef_linear * identity + coef_cubic * power + coef_quintic * mul(power, power)


def small_rows(rows_own, rows_all, hidden, groups):
    outer = lax.dot_general(rows_all, rows_all, cols_last, preferred_element_type=jnp.float32)
    hid = lax.dot_general(hidden, hidden, cols_last, preferred_element_type=jnp.float32)
    total = jnp.maximum(jnp.sum(outer * hid), 0.0) / (groups * groups)
    scale = 1.0 / (groups * (jnp.sqrt(total) + norm_eps))
    power = mul(hid * scale, outer * scale)
    identity = jnp.eye(power.shape[0], dtype=jnp.float32)
    left = rows_own.astype(jnp.float32).T * scale
    for step in range(ITERS):
        step_factor = factor(power, identity)
        left = mul(left, step_factor)
        if step < ITERS - 1:
            power = mul(mul(power, step_factor), step_factor)
    return mul(left, hidden.astype(jnp.float32))


def small_units(rows_own, rows_all, hidden, groups):
    whole = lax.dot_general(rows_all, hidden, rows_first, preferred_element_type=jnp.float32) / groups
    own = lax.dot_general(rows_own, hidden, rows_first, preferred_element_type=jnp.float32) / groups
    norm = jnp.sqrt(jnp.sum(whole * whole)) + norm_eps
    whole = whole / norm
    own = own / norm
    power = lax.dot_general(
        whole, whole, rows_first, precision=high, preferred_element_type=jnp.float32
    )
    identity = jnp.eye(power.shape[0], dtype=jnp.float32)
    for step in range(ITERS):
        step_factor = factor(power, identity)
        own = mul(own, step_factor)
        if step < ITERS - 1:
            power = mul(mul(power, step_factor), step_factor)
    return own


rows_cols = (((1,), (0,)), ((), ()))


def dot(left, right, dims=rows_cols):
    return lax.dot_general(left, right, dims, preferred_element_type=jnp.float32)


def split(value):
    top = value.astype(jnp.bfloat16)
    return top, (value - top.astype(jnp.float32)).astype(jnp.bfloat16)


def dot3(left, right):
    return dot(left[0], right[0]) + (dot(left[0], right[1]) + dot(left[1], right[0]))


def remote(src, dst, send, recv, device):
    return pltpu.make_async_remote_copy(
        src_ref=src, dst_ref=dst, send_sem=send, recv_sem=recv,
        device_id=device, device_id_type=pl.DeviceIdType.MESH,
    )


def kernel(
    owners, groups,
    inputs_hbm, grad_hbm, routes, gate_probs, gate_hbm, up_hbm, down_hbm,
    slots_out, left_out, h_out, d_out, x_out, ret_out,
    inputs, out_grad, w_gate, w_up, w_down, x_send, g_send, x_recv, s_all, h_all, d_all, x_own, back_send, ret,
    w_sem, xs_sem, xr_sem, gs_sem, gr_sem, bs_sem, br_sem,
    o_sem, os_sem, or_sem, ss_sem, sr_sem, hs_sem, hr_sem, ds_sem, dr_sem,
):
    me = lax.axis_index("ep")
    rep = lax.axis_index("rep")
    core = rep % 2
    chip = rep // 2
    chips = groups // 2
    sibling = chip * 2 + (1 - core)
    tokens, width = inputs.shape
    units = h_all.shape[2]
    rows = owners * CAP
    share = width // groups
    if owners == 4:
        near = [me + 1 - 2 * (me % 2), (me + 2) % 4, 3 - me]
    else:
        near = [(me + k) % owners for k in range(1, owners)]
    far = [((chip + k) % chips) * 2 + core for k in range(1, chips)]
    others = [(rep + k) % groups for k in range(1, groups)]

    barrier = pltpu.get_barrier_semaphore()
    for peer in near:
        pl.semaphore_signal(barrier, inc=1, device_id={"ep": peer}, device_id_type=pl.DeviceIdType.MESH)
    for peer in others:
        pl.semaphore_signal(barrier, inc=1, device_id={"rep": peer}, device_id_type=pl.DeviceIdType.MESH)

    loads = [
        pltpu.make_async_copy(src, dst, w_sem.at[n])
        for n, (src, dst) in enumerate(((gate_hbm.at[0], w_gate), (up_hbm.at[0], w_up), (down_hbm.at[0], w_down),
        (inputs_hbm, inputs), (grad_hbm, out_grad)))
    ]
    for n in (3, 4, 0, 1, 2):
        loads[n].start()
    line = lax.broadcasted_iota(jnp.int32, (rows, tokens), 0)
    place = (line % CAP).astype(jnp.float32)
    expert = line // CAP
    named = jnp.zeros((rows, tokens), jnp.float32)
    weight = jnp.zeros((rows, tokens), jnp.float32)
    for k in range(routes.shape[0]):
        hit = routes[k : k + 1, :] == expert
        named = named + jnp.where(hit, 1.0, 0.0)
        weight = weight + jnp.where(hit, gate_probs[k : k + 1, :], 0.0)
    earlier = lax.broadcasted_iota(jnp.int32, (tokens, tokens), 0) < lax.broadcasted_iota(
        jnp.int32, (tokens, tokens), 1
    )
    before = dot(named.astype(jnp.bfloat16), jnp.where(earlier, 1.0, 0.0).astype(jnp.bfloat16))
    slots = jnp.where(before == place, named, 0.0)
    dispatch = slots.astype(jnp.bfloat16)
    slots_out[...] = dispatch
    weight = jnp.sum(slots * weight, axis=1, keepdims=True)
    loads[3].wait()
    x_send[...] = dot(dispatch, inputs[...]).astype(jnp.bfloat16).reshape(owners, CAP, width)
    pl.semaphore_wait(barrier, len(near) + len(others))
    sends = []

    def send(*spec):
        copy = remote(*spec)
        copy.start()
        sends.append(copy)

    for n, peer in enumerate(near):
        send(x_send.at[peer], x_recv.at[me], xs_sem.at[n], xr_sem.at[me], {"ep": peer})
    loads[4].wait()
    g_send[...] = (dot(dispatch, out_grad[...]) * weight).astype(jnp.bfloat16).reshape(owners, CAP, width)
    for n, peer in enumerate(near):
        send(g_send.at[peer], s_all.at[rep, me], gs_sem.at[n], gr_sem.at[me], {"ep": peer})
    x_recv[me] = x_send[me]
    s_all[rep, me] = g_send[me]

    def arrived(ref, recv, peer):
        remote(ref, ref, xs_sem.at[0], recv, {"ep": peer}).wait_recv()

    def piece(j):
        block = s_all.at[rep, j]
        for n, peer in enumerate(far):
            send(block, block, ss_sem.at[n, j], sr_sem.at[rep, j], {"rep": peer})
        send(block, block, ss_sem.at[len(far), j], sr_sem.at[rep, j], {"rep": sibling})

    piece(me)

    def spread(ref, send_sem, recv_sem):
        for n, peer in enumerate(far):
            send(ref.at[rep], ref.at[rep], send_sem.at[n], recv_sem.at[rep], {"rep": peer})
        send(ref.at[rep], ref.at[rep], send_sem.at[len(far)], recv_sem.at[rep], {"rep": sibling})

    def swap(ref, send_sem, recv_sem):
        for n, peer in enumerate(far):
            arrived(ref.at[peer], recv_sem.at[peer], near[0])
            send(ref.at[peer], ref.at[peer], send_sem.at[chips + n], recv_sem.at[peer], {"rep": sibling})

    def finish(ref, recv_sem):
        for k in range(chips):
            source = ((chip + k) % chips) * 2 + (1 - core)
            arrived(ref.at[source], recv_sem.at[source], near[0])

    for peer in near:
        arrived(x_recv.at[peer], xr_sem.at[peer], peer)
    for n, peer in enumerate(others):
        columns = pl.ds(pl.multiple_of(peer * share, 128), share)
        send(x_recv.at[:, :, columns], x_own.at[rep], os_sem.at[n], or_sem.at[rep], {"rep": peer})
    loads[0].wait()
    loads[1].wait()
    x = x_recv[...].reshape(rows, width)
    pre_gate = dot(x, w_gate[...])
    pre_up = dot(x, w_up[...])
    sigma = jax.nn.sigmoid(pre_gate)
    swish = pre_gate * sigma
    h_all[rep] = (swish * pre_up).astype(jnp.bfloat16)
    spread(h_all, hs_sem, hr_sem)
    loads[2].wait()
    for peer in near:
        arrived(s_all.at[rep, peer], gr_sem.at[peer], peer)
        piece(peer)
    d_hidden = dot(s_all[rep].reshape(rows, width), w_down[...], cols_last)
    d_up = (d_hidden * swish).astype(jnp.bfloat16)
    d_gate = (d_hidden * pre_up * sigma * (1.0 + pre_gate * (1.0 - sigma))).astype(jnp.bfloat16)
    d_all[rep, :, :units] = d_gate
    d_all[rep, :, units:] = d_up
    mine = pl.ds(pl.multiple_of(rep * share, 128), share)
    x_own[rep] = x_recv[:, :, mine]
    swap(h_all, hs_sem, hr_sem)
    back = dot(d_gate, w_gate[...], cols_last) + dot(d_up, w_up[...], cols_last)
    back_send[...] = back.astype(jnp.bfloat16).reshape(owners, CAP, width)
    for n, peer in enumerate(near):
        send(back_send.at[peer], ret.at[me], bs_sem.at[n], br_sem.at[me], {"ep": peer})
    ret[me] = back_send[me]
    finish(h_all, hr_sem)
    stores = [
        pltpu.make_async_copy(src, dst, o_sem.at[n])
        for n, (src, dst) in enumerate(((h_all, h_out), (ret, ret_out), (x_own, x_out), (d_all, d_out)))
    ]
    stores[0].start()
    hidden = h_all[...].reshape(groups * rows, units)
    hid = dot(hidden, hidden, cols_last)
    for j in [me] + near:
        for n, peer in enumerate(far):
            block = s_all.at[peer, j]
            arrived(block, sr_sem.at[peer, j], near[0])
            send(block, block, ss_sem.at[chips + n, j], sr_sem.at[peer, j], {"rep": sibling})
    spread(d_all, ds_sem, dr_sem)
    for j in [me] + near:
        for k in range(chips):
            source = ((chip + k) % chips) * 2 + (1 - core)
            arrived(s_all.at[source, j], sr_sem.at[source, j], near[0])
    scaled = s_all[...].reshape(groups * rows, width)
    outer = dot(scaled, scaled, cols_last)
    total = jnp.sum(jnp.sum(outer * hid, axis=0, keepdims=True), axis=1, keepdims=True)
    total = jnp.maximum(total, 0.0) / (groups * groups)
    scale = 1.0 / (groups * (jnp.sqrt(total) + norm_eps))
    power = dot3(split(outer * scale), split(hid * scale))
    left = s_all[:, :, :, mine].reshape(groups * rows, share).astype(jnp.float32) * scale
    size = groups * rows
    diagonal = lax.broadcasted_iota(jnp.int32, (size, size), 0) == lax.broadcasted_iota(
        jnp.int32, (size, size), 1
    )
    for step in range(ITERS - 1):
        parts = split(power)
        poly = coef_cubic * power + coef_quintic * dot3(parts, parts)
        poly = split(poly + jnp.where(diagonal, coef_linear, 0.0))
        left = dot3(poly, split(left))
        power = dot3(split(dot3(parts, poly)), poly)
    swap(d_all, ds_sem, dr_sem)
    parts = split(power)
    left = coef_linear * left + dot3(
        parts, split(coef_cubic * left + coef_quintic * dot3(parts, split(left)))
    )
    top, rest = split(left)
    left_out[0] = top
    left_out[1] = rest
    for peer in near:
        arrived(ret.at[peer], br_sem.at[peer], peer)
    stores[1].start()
    for peer in others:
        arrived(x_own.at[peer], or_sem.at[peer], near[0])
    stores[2].start()
    finish(d_all, dr_sem)
    stores[3].start()
    for store in stores:
        store.wait()
    for copy in sends:
        copy.wait_send()


def products(groups, slots, ret, left, x_own, hidden, d_gate, d_up, input_grad, gate_grad, up_grad, down_update):
    @pl.when(pl.program_id(0) == 0)
    def _():
        input_grad[...] = dot(slots[...], ret[...], rows_first).astype(jnp.bfloat16)

    gate_grad[0] = dot(x_own[...], d_gate[...], rows_first) / groups
    up_grad[0] = dot(x_own[...], d_up[...], rows_first) / groups
    down_update[0] = dot(left[0], hidden[...], rows_first) + dot(left[1], hidden[...], rows_first)


def fused(inputs, out_grad, routes, gate_probs, gate_weight, up_weight, down_weight):
    owners = lax.axis_size("ep")
    groups = lax.axis_size("rep")
    tokens, width = inputs.shape
    units = gate_weight.shape[2]
    rows = owners * CAP
    share = width // groups
    chips = groups // 2
    half = jnp.bfloat16
    inside = pl.BlockSpec(memory_space=pltpu.VMEM)
    outside = pl.BlockSpec(memory_space=pl.ANY)
    dma = pltpu.SemaphoreType.DMA
    shapes = [(rows, tokens), (2, groups * rows, share), (groups, rows, units),
              (groups, rows, 2 * units), (groups, owners, CAP, share), (owners, CAP, width)]
    slots, left, h_all, d_all, x_own, ret = pl.pallas_call(
        functools.partial(kernel, owners, groups),
        out_shape=[jax.ShapeDtypeStruct(shape, half) for shape in shapes],
        in_specs=[outside] * 2 + [inside] * 2 + [outside] * 3,
        out_specs=[inside] * 2 + [outside] * 4,
        scratch_shapes=[
            pltpu.VMEM((tokens, width), half),
            pltpu.VMEM((tokens, width), half),
            pltpu.VMEM((width, units), half),
            pltpu.VMEM((width, units), half),
            pltpu.VMEM((units, width), half),
            pltpu.VMEM((owners, CAP, width), half),
            pltpu.VMEM((owners, CAP, width), half),
            pltpu.VMEM((owners, CAP, width), half),
            pltpu.VMEM((groups, owners, CAP, width), half),
            pltpu.VMEM((groups, rows, units), half),
            pltpu.VMEM((groups, rows, 2 * units), half),
            pltpu.VMEM((groups, owners, CAP, share), half),
            pltpu.VMEM((owners, CAP, width), half),
            pltpu.VMEM((owners, CAP, width), half),
            dma((5,)),
        ]
        + [dma((owners,))] * 6
        + [dma((4,))]
        + [dma((groups,))] * 2
        + [dma((groups, owners))] * 2
        + [dma((groups,))] * 4,
        compiler_params=pltpu.CompilerParams(
            collective_id=0, has_side_effects=True, vmem_limit_bytes=62 * 1024 * 1024
        ),
    )(inputs, out_grad, routes.T, gate_probs.T, gate_weight, up_weight, down_weight)
    total = groups * rows
    block = 256 if units % 256 == 0 else units
    steps = units // block
    d_rows = d_all.reshape(total, 2 * units)
    fixed = lambda i: (0, 0)
    return pl.pallas_call(
        functools.partial(products, groups),
        grid=(steps,),
        out_shape=(jax.ShapeDtypeStruct((tokens, width), half),)
        + (jax.ShapeDtypeStruct((1, share, units), jnp.float32),) * 3,
        in_specs=[
            pl.BlockSpec((rows, tokens), fixed),
            pl.BlockSpec((rows, width), fixed),
            pl.BlockSpec((2, total, share), lambda i: (0, 0, 0)),
            pl.BlockSpec((total, share), fixed),
            pl.BlockSpec((total, block), lambda i: (0, i)),
            pl.BlockSpec((total, block), lambda i: (0, i)),
            pl.BlockSpec((total, block), lambda i: (0, i + steps)),
        ],
        out_specs=(pl.BlockSpec((tokens, width), fixed),)
        + (pl.BlockSpec((1, share, block), lambda i: (0, 0, i)),) * 3,
    )(slots, ret.reshape(rows, width), left, x_own.reshape(total, share),
      h_all.reshape(total, units), d_rows, d_rows)


def per_device(inputs, out_grad, routes, gate_probs, gate_weight, up_weight, down_weight):
    owners = lax.axis_size("ep")
    groups = lax.axis_size("rep")
    width = inputs.shape[1]
    rows = owners * CAP
    if groups * rows < gate_weight.shape[2] and rows <= 128 and groups % 2 == 0:
        return fused(inputs, out_grad, routes, gate_probs, gate_weight, up_weight, down_weight)
    dispatch, weight = slot_tables(routes, gate_probs, owners, CAP)
    rows_send = jnp.dot(dispatch, inputs, preferred_element_type=jnp.float32).astype(jnp.bfloat16)
    grad_send = jnp.dot(dispatch, out_grad, preferred_element_type=jnp.float32) * weight[:, None]
    grad_send = grad_send.astype(jnp.bfloat16)
    both_send = jnp.concatenate([rows_send, grad_send], axis=1)
    both_recv = lax.all_to_all(
        both_send.reshape(owners, CAP, 2 * width), "ep", split_axis=0, concat_axis=0, tiled=True
    ).reshape(rows, 2 * width)
    rows_recv = both_recv[:, :width]
    scaled = both_recv[:, width:]
    scaled_all = lax.all_gather(scaled, "rep", axis=0, tiled=True)
    rows_own = lax.all_to_all(
        rows_recv.reshape(rows, groups, width // groups).transpose(1, 0, 2),
        "rep", split_axis=0, concat_axis=0, tiled=True,
    ).reshape(groups * rows, width // groups)
    w_gate = gate_weight[0]
    w_up = up_weight[0]
    w_down = down_weight[0]
    units = w_gate.shape[1]
    pre_gate = jnp.dot(rows_recv, w_gate, preferred_element_type=jnp.float32)
    pre_up = jnp.dot(rows_recv, w_up, preferred_element_type=jnp.float32)
    sigma = jax.nn.sigmoid(pre_gate)
    swish = pre_gate * sigma
    hidden = (swish * pre_up).astype(jnp.bfloat16)
    d_hidden = lax.dot_general(scaled, w_down, cols_last, preferred_element_type=jnp.float32)
    d_up = (d_hidden * swish).astype(jnp.bfloat16)
    d_gate = (d_hidden * pre_up * sigma * (1.0 + pre_gate * (1.0 - sigma))).astype(jnp.bfloat16)
    back = lax.dot_general(d_gate, w_gate, cols_last, preferred_element_type=jnp.float32)
    back = (
        back + lax.dot_general(d_up, w_up, cols_last, preferred_element_type=jnp.float32)
    ).astype(jnp.bfloat16)
    returned = lax.all_to_all(
        back.reshape(owners, CAP, width), "ep", split_axis=0, concat_axis=0, tiled=True
    ).reshape(owners * CAP, width)
    input_grad = lax.dot_general(
        dispatch, returned, rows_first, preferred_element_type=jnp.float32
    ).astype(jnp.bfloat16)
    units_all = lax.all_gather(
        jnp.concatenate([d_gate, d_up, hidden], axis=1), "rep", axis=0, tiled=True
    )
    both = lax.dot_general(
        rows_own, units_all[:, : 2 * units], rows_first, preferred_element_type=jnp.float32
    ) / groups
    gate_grad = both[:, :units]
    up_grad = both[:, units:]
    hidden_all = units_all[:, 2 * units :]
    share = width // groups
    scaled_own = lax.dynamic_slice_in_dim(scaled_all, lax.axis_index("rep") * share, share, axis=1)
    form = small_rows if groups * rows < units else small_units
    down_update = form(scaled_own, scaled_all, hidden_all, groups)
    return (input_grad, gate_grad[None], up_grad[None], down_update[None])


def solution(mesh):
    in_specs = (
        P(("rep", "ep"), None),
        P(("rep", "ep"), None),
        P(("rep", "ep"), None),
        P(("rep", "ep"), None),
        P("ep", None, None),
        P("ep", None, None),
        P("ep", None, None),
    )
    out_specs = (
        P(("rep", "ep"), None),
        P("ep", "rep", None),
        P("ep", "rep", None),
        P("ep", "rep", None),
    )
    return jax.shard_map(
        per_device, mesh=mesh, in_specs=in_specs, out_specs=out_specs, check_vma=False
    )
```

```python
import functools

import jax
import jax.numpy as jnp
from jax import lax
from jax.experimental import pallas as pl
from jax.experimental.pallas import tpu as pltpu
from jax.sharding import PartitionSpec as P

ITERS = 3
CAP = 16


coef_linear = 3.4445
coef_cubic = -4.775
coef_quintic = 2.0315
norm_eps = 1e-06
rows_first = (((0,), (0,)), ((), ()))
cols_last = (((1,), (1,)), ((), ()))


def slot_tables(routes, gate_probs, owners, capacity):
    count, picks = routes.shape
    flat = routes.reshape(count * picks)
    labels = jnp.arange(owners, dtype=jnp.int32)
    onehot = (flat[:, None] == labels[None, :]).astype(jnp.int32)
    before = jnp.cumsum(onehot, axis=0) - onehot
    place = jnp.sum(before * onehot, axis=1)
    target = jnp.where(flat < owners, flat * capacity + place, -1)
    slots = jnp.arange(owners * capacity, dtype=jnp.int32)
    match = (target[None, :] == slots[:, None]).reshape(owners * capacity, count, picks)
    dispatch = jnp.sum(match.astype(jnp.float32), axis=2).astype(jnp.bfloat16)
    weight = jnp.sum(jnp.where(match, gate_probs[None, :, :], jnp.float32(0.0)), axis=(1, 2))
    return (dispatch, weight)


high = lax.Precision.HIGH


def mul(left, right):
    return jnp.dot(left, right, precision=high, preferred_element_type=jnp.float32)


def factor(power, identity):
    return coef_linear * identity + coef_cubic * power + coef_quintic * mul(power, power)


def small_rows(rows_own, rows_all, hidden, groups):
    outer = lax.dot_general(rows_all, rows_all, cols_last, preferred_element_type=jnp.float32)
    hid = lax.dot_general(hidden, hidden, cols_last, preferred_element_type=jnp.float32)
    total = jnp.maximum(jnp.sum(outer * hid), 0.0) / (groups * groups)
    scale = 1.0 / (groups * (jnp.sqrt(total) + norm_eps))
    power = mul(hid * scale, outer * scale)
    identity = jnp.eye(power.shape[0], dtype=jnp.float32)
    left = rows_own.astype(jnp.float32).T * scale
    for step in range(ITERS):
        step_factor = factor(power, identity)
        left = mul(left, step_factor)
        if step < ITERS - 1:
            power = mul(mul(power, step_factor), step_factor)
    return mul(left, hidden.astype(jnp.float32))


def small_units(rows_own, rows_all, hidden, groups):
    whole = lax.dot_general(rows_all, hidden, rows_first, preferred_element_type=jnp.float32) / groups
    own = lax.dot_general(rows_own, hidden, rows_first, preferred_element_type=jnp.float32) / groups
    norm = jnp.sqrt(jnp.sum(whole * whole)) + norm_eps
    whole = whole / norm
    own = own / norm
    power = lax.dot_general(
        whole, whole, rows_first, precision=high, preferred_element_type=jnp.float32
    )
    identity = jnp.eye(power.shape[0], dtype=jnp.float32)
    for step in range(ITERS):
        step_factor = factor(power, identity)
        own = mul(own, step_factor)
        if step < ITERS - 1:
            power = mul(mul(power, step_factor), step_factor)
    return own


rows_cols = (((1,), (0,)), ((), ()))


def dot(left, right, dims=rows_cols):
    return lax.dot_general(left, right, dims, preferred_element_type=jnp.float32)


def split(value):
    top = value.astype(jnp.bfloat16)
    return top, (value - top.astype(jnp.float32)).astype(jnp.bfloat16)


def dot3(left, right):
    wide = jnp.concatenate([left[0], left[0], left[1]], axis=1)
    tall = jnp.concatenate([right[0], right[1], right[0]], axis=0)
    return dot(wide, tall)


def remote(src, dst, send, recv, device):
    return pltpu.make_async_remote_copy(
        src_ref=src, dst_ref=dst, send_sem=send, recv_sem=recv,
        device_id=device, device_id_type=pl.DeviceIdType.MESH,
    )


def kernel(
    owners, groups,
    inputs_hbm, grad_hbm, routes, gate_probs, gate_hbm, up_hbm, down_hbm,
    slots_out, left_out, h_out, d_out, x_out, ret_out,
    inputs, out_grad, w_gate, w_up, w_down, x_send, g_send, x_recv, s_all, h_all, d_all, x_own, back_send, ret,
    w_sem, xs_sem, xr_sem, gs_sem, gr_sem, bs_sem, br_sem,
    o_sem, os_sem, or_sem, ss_sem, sr_sem, hs_sem, hr_sem, ds_sem, dr_sem,
):
    me = lax.axis_index("ep")
    rep = lax.axis_index("rep")
    core = rep % 2
    chip = rep // 2
    chips = groups // 2
    sibling = chip * 2 + (1 - core)
    tokens, width = inputs.shape
    units = h_all.shape[2]
    rows = owners * CAP
    share = width // groups
    if owners == 4:
        near = [me + 1 - 2 * (me % 2), (me + 2) % 4, 3 - me]
    else:
        near = [(me + k) % owners for k in range(1, owners)]
    far = [((chip + k) % chips) * 2 + core for k in range(1, chips)]
    others = [(rep + k) % groups for k in range(1, groups)]

    barrier = pltpu.get_barrier_semaphore()
    for peer in near:
        pl.semaphore_signal(barrier, inc=1, device_id={"ep": peer}, device_id_type=pl.DeviceIdType.MESH)
    for peer in others:
        pl.semaphore_signal(barrier, inc=1, device_id={"rep": peer}, device_id_type=pl.DeviceIdType.MESH)

    loads = [
        pltpu.make_async_copy(src, dst, w_sem.at[n])
        for n, (src, dst) in enumerate(((gate_hbm.at[0], w_gate), (up_hbm.at[0], w_up), (down_hbm.at[0], w_down),
        (inputs_hbm, inputs), (grad_hbm, out_grad)))
    ]
    for n in (3, 4, 0, 1, 2):
        loads[n].start()
    line = lax.broadcasted_iota(jnp.int32, (rows, tokens), 0)
    place = (line % CAP).astype(jnp.float32)
    expert = line // CAP
    named = jnp.zeros((rows, tokens), jnp.float32)
    weight = jnp.zeros((rows, tokens), jnp.float32)
    for k in range(routes.shape[0]):
        hit = routes[k : k + 1, :] == expert
        named = named + jnp.where(hit, 1.0, 0.0)
        weight = weight + jnp.where(hit, gate_probs[k : k + 1, :], 0.0)
    earlier = lax.broadcasted_iota(jnp.int32, (tokens, tokens), 0) < lax.broadcasted_iota(
        jnp.int32, (tokens, tokens), 1
    )
    before = dot(named.astype(jnp.bfloat16), jnp.where(earlier, 1.0, 0.0).astype(jnp.bfloat16))
    slots = jnp.where(before == place, named, 0.0)
    dispatch = slots.astype(jnp.bfloat16)
    slots_out[...] = dispatch
    weight = jnp.sum(slots * weight, axis=1, keepdims=True)
    loads[3].wait()
    x_send[...] = dot(dispatch, inputs[...]).astype(jnp.bfloat16).reshape(owners, CAP, width)
    pl.semaphore_wait(barrier, len(near) + len(others))
    sends = []

    def send(*spec):
        copy = remote(*spec)
        copy.start()
        sends.append(copy)

    for n, peer in enumerate(near):
        send(x_send.at[peer], x_recv.at[me], xs_sem.at[n], xr_sem.at[me], {"ep": peer})
    loads[4].wait()
    g_send[...] = (dot(dispatch, out_grad[...]) * weight).astype(jnp.bfloat16).reshape(owners, CAP, width)
    for n, peer in enumerate(near):
        send(g_send.at[peer], s_all.at[rep, me], gs_sem.at[n], gr_sem.at[me], {"ep": peer})
    x_recv[me] = x_send[me]
    s_all[rep, me] = g_send[me]

    def arrived(ref, recv, peer):
        remote(ref, ref, xs_sem.at[0], recv, {"ep": peer}).wait_recv()

    def piece(j):
        block = s_all.at[rep, j]
        for n, peer in enumerate(far):
            send(block, block, ss_sem.at[n, j], sr_sem.at[rep, j], {"rep": peer})
        send(block, block, ss_sem.at[len(far), j], sr_sem.at[rep, j], {"rep": sibling})

    piece(me)

    def spread(ref, send_sem, recv_sem):
        for n, peer in enumerate(far):
            send(ref.at[rep], ref.at[rep], send_sem.at[n], recv_sem.at[rep], {"rep": peer})
        send(ref.at[rep], ref.at[rep], send_sem.at[len(far)], recv_sem.at[rep], {"rep": sibling})

    def swap(ref, send_sem, recv_sem):
        for n, peer in enumerate(far):
            arrived(ref.at[peer], recv_sem.at[peer], near[0])
            send(ref.at[peer], ref.at[peer], send_sem.at[chips + n], recv_sem.at[peer], {"rep": sibling})

    def finish(ref, recv_sem):
        for k in range(chips):
            source = ((chip + k) % chips) * 2 + (1 - core)
            arrived(ref.at[source], recv_sem.at[source], near[0])

    for peer in near:
        arrived(x_recv.at[peer], xr_sem.at[peer], peer)
    for n, peer in enumerate(others):
        columns = pl.ds(pl.multiple_of(peer * share, 128), share)
        send(x_recv.at[:, :, columns], x_own.at[rep], os_sem.at[n], or_sem.at[rep], {"rep": peer})
    loads[0].wait()
    loads[1].wait()
    x = x_recv[...].reshape(rows, width)
    pre_gate = dot(x, w_gate[...])
    pre_up = dot(x, w_up[...])
    sigma = jax.nn.sigmoid(pre_gate)
    swish = pre_gate * sigma
    h_all[rep] = (swish * pre_up).astype(jnp.bfloat16)
    spread(h_all, hs_sem, hr_sem)
    loads[2].wait()
    for peer in near:
        arrived(s_all.at[rep, peer], gr_sem.at[peer], peer)
        piece(peer)
    d_hidden = dot(s_all[rep].reshape(rows, width), w_down[...], cols_last)
    d_up = (d_hidden * swish).astype(jnp.bfloat16)
    d_gate = (d_hidden * pre_up * sigma * (1.0 + pre_gate * (1.0 - sigma))).astype(jnp.bfloat16)
    d_all[rep, :, :units] = d_gate
    d_all[rep, :, units:] = d_up
    mine = pl.ds(pl.multiple_of(rep * share, 128), share)
    x_own[rep] = x_recv[:, :, mine]
    swap(h_all, hs_sem, hr_sem)
    back = dot(d_gate, w_gate[...], cols_last) + dot(d_up, w_up[...], cols_last)
    back_send[...] = back.astype(jnp.bfloat16).reshape(owners, CAP, width)
    for n, peer in enumerate(near):
        send(back_send.at[peer], ret.at[me], bs_sem.at[n], br_sem.at[me], {"ep": peer})
    ret[me] = back_send[me]
    finish(h_all, hr_sem)
    stores = [
        pltpu.make_async_copy(src, dst, o_sem.at[n])
        for n, (src, dst) in enumerate(((h_all, h_out), (ret, ret_out), (x_own, x_out), (d_all, d_out)))
    ]
    stores[0].start()
    hidden = h_all[...].reshape(groups * rows, units)
    hid = dot(hidden, hidden, cols_last)
    for j in [me] + near:
        for n, peer in enumerate(far):
            block = s_all.at[peer, j]
            arrived(block, sr_sem.at[peer, j], near[0])
            send(block, block, ss_sem.at[chips + n, j], sr_sem.at[peer, j], {"rep": sibling})
    spread(d_all, ds_sem, dr_sem)
    for j in [me] + near:
        for k in range(chips):
            source = ((chip + k) % chips) * 2 + (1 - core)
            arrived(s_all.at[source, j], sr_sem.at[source, j], near[0])
    scaled = s_all[...].reshape(groups * rows, width)
    outer = dot(scaled, scaled, cols_last)
    total = jnp.sum(jnp.sum(outer * hid, axis=0, keepdims=True), axis=1, keepdims=True)
    total = jnp.maximum(total, 0.0) / (groups * groups)
    scale = 1.0 / (groups * (jnp.sqrt(total) + norm_eps))
    power = dot3(split(outer * scale), split(hid * scale))
    left = s_all[:, :, :, mine].reshape(groups * rows, share).astype(jnp.float32) * scale
    size = groups * rows
    diagonal = lax.broadcasted_iota(jnp.int32, (size, size), 0) == lax.broadcasted_iota(
        jnp.int32, (size, size), 1
    )
    for step in range(ITERS - 1):
        parts = split(power)
        poly = coef_cubic * power + coef_quintic * dot3(parts, parts)
        poly = split(poly + jnp.where(diagonal, coef_linear, 0.0))
        left = dot3(poly, split(left))
        power = dot3(split(dot3(parts, poly)), poly)
    swap(d_all, ds_sem, dr_sem)
    parts = split(power)
    left = coef_linear * left + dot3(
        parts, split(coef_cubic * left + coef_quintic * dot3(parts, split(left)))
    )
    top, rest = split(left)
    left_out[0] = top
    left_out[1] = rest
    for peer in near:
        arrived(ret.at[peer], br_sem.at[peer], peer)
    stores[1].start()
    for peer in others:
        arrived(x_own.at[peer], or_sem.at[peer], near[0])
    stores[2].start()
    finish(d_all, dr_sem)
    stores[3].start()
    for store in stores:
        store.wait()
    for copy in sends:
        copy.wait_send()


def products(groups, slots, ret, left, x_own, hidden, d_gate, d_up, input_grad, gate_grad, up_grad, down_update):
    @pl.when(pl.program_id(0) == 0)
    def _():
        input_grad[...] = dot(slots[...], ret[...], rows_first).astype(jnp.bfloat16)

    gate_grad[0] = dot(x_own[...], d_gate[...], rows_first) / groups
    up_grad[0] = dot(x_own[...], d_up[...], rows_first) / groups
    down_update[0] = dot(left[0], hidden[...], rows_first) + dot(left[1], hidden[...], rows_first)


def fused(inputs, out_grad, routes, gate_probs, gate_weight, up_weight, down_weight):
    owners = lax.axis_size("ep")
    groups = lax.axis_size("rep")
    tokens, width = inputs.shape
    units = gate_weight.shape[2]
    rows = owners * CAP
    share = width // groups
    chips = groups // 2
    half = jnp.bfloat16
    inside = pl.BlockSpec(memory_space=pltpu.VMEM)
    outside = pl.BlockSpec(memory_space=pl.ANY)
    dma = pltpu.SemaphoreType.DMA
    shapes = [(rows, tokens), (2, groups * rows, share), (groups, rows, units),
              (groups, rows, 2 * units), (groups, owners, CAP, share), (owners, CAP, width)]
    slots, left, h_all, d_all, x_own, ret = pl.pallas_call(
        functools.partial(kernel, owners, groups),
        out_shape=[jax.ShapeDtypeStruct(shape, half) for shape in shapes],
        in_specs=[outside] * 2 + [inside] * 2 + [outside] * 3,
        out_specs=[inside] * 2 + [outside] * 4,
        scratch_shapes=[
            pltpu.VMEM((tokens, width), half),
            pltpu.VMEM((tokens, width), half),
            pltpu.VMEM((width, units), half),
            pltpu.VMEM((width, units), half),
            pltpu.VMEM((units, width), half),
            pltpu.VMEM((owners, CAP, width), half),
            pltpu.VMEM((owners, CAP, width), half),
            pltpu.VMEM((owners, CAP, width), half),
            pltpu.VMEM((groups, owners, CAP, width), half),
            pltpu.VMEM((groups, rows, units), half),
            pltpu.VMEM((groups, rows, 2 * units), half),
            pltpu.VMEM((groups, owners, CAP, share), half),
            pltpu.VMEM((owners, CAP, width), half),
            pltpu.VMEM((owners, CAP, width), half),
            dma((5,)),
        ]
        + [dma((owners,))] * 6
        + [dma((4,))]
        + [dma((groups,))] * 2
        + [dma((groups, owners))] * 2
        + [dma((groups,))] * 4,
        compiler_params=pltpu.CompilerParams(
            collective_id=0, has_side_effects=True, vmem_limit_bytes=62 * 1024 * 1024
        ),
    )(inputs, out_grad, routes.T, gate_probs.T, gate_weight, up_weight, down_weight)
    total = groups * rows
    block = 256 if units % 256 == 0 else units
    steps = units // block
    d_rows = d_all.reshape(total, 2 * units)
    fixed = lambda i: (0, 0)
    return pl.pallas_call(
        functools.partial(products, groups),
        grid=(steps,),
        out_shape=(jax.ShapeDtypeStruct((tokens, width), half),)
        + (jax.ShapeDtypeStruct((1, share, units), jnp.float32),) * 3,
        in_specs=[
            pl.BlockSpec((rows, tokens), fixed),
            pl.BlockSpec((rows, width), fixed),
            pl.BlockSpec((2, total, share), lambda i: (0, 0, 0)),
            pl.BlockSpec((total, share), fixed),
            pl.BlockSpec((total, block), lambda i: (0, i)),
            pl.BlockSpec((total, block), lambda i: (0, i)),
            pl.BlockSpec((total, block), lambda i: (0, i + steps)),
        ],
        out_specs=(pl.BlockSpec((tokens, width), fixed),)
        + (pl.BlockSpec((1, share, block), lambda i: (0, 0, i)),) * 3,
    )(slots, ret.reshape(rows, width), left, x_own.reshape(total, share),
      h_all.reshape(total, units), d_rows, d_rows)


def per_device(inputs, out_grad, routes, gate_probs, gate_weight, up_weight, down_weight):
    owners = lax.axis_size("ep")
    groups = lax.axis_size("rep")
    width = inputs.shape[1]
    rows = owners * CAP
    if groups * rows < gate_weight.shape[2] and rows <= 128 and groups % 2 == 0:
        return fused(inputs, out_grad, routes, gate_probs, gate_weight, up_weight, down_weight)
    dispatch, weight = slot_tables(routes, gate_probs, owners, CAP)
    rows_send = jnp.dot(dispatch, inputs, preferred_element_type=jnp.float32).astype(jnp.bfloat16)
    grad_send = jnp.dot(dispatch, out_grad, preferred_element_type=jnp.float32) * weight[:, None]
    grad_send = grad_send.astype(jnp.bfloat16)
    both_send = jnp.concatenate([rows_send, grad_send], axis=1)
    both_recv = lax.all_to_all(
        both_send.reshape(owners, CAP, 2 * width), "ep", split_axis=0, concat_axis=0, tiled=True
    ).reshape(rows, 2 * width)
    rows_recv = both_recv[:, :width]
    scaled = both_recv[:, width:]
    scaled_all = lax.all_gather(scaled, "rep", axis=0, tiled=True)
    rows_own = lax.all_to_all(
        rows_recv.reshape(rows, groups, width // groups).transpose(1, 0, 2),
        "rep", split_axis=0, concat_axis=0, tiled=True,
    ).reshape(groups * rows, width // groups)
    w_gate = gate_weight[0]
    w_up = up_weight[0]
    w_down = down_weight[0]
    units = w_gate.shape[1]
    pre_gate = jnp.dot(rows_recv, w_gate, preferred_element_type=jnp.float32)
    pre_up = jnp.dot(rows_recv, w_up, preferred_element_type=jnp.float32)
    sigma = jax.nn.sigmoid(pre_gate)
    swish = pre_gate * sigma
    hidden = (swish * pre_up).astype(jnp.bfloat16)
    d_hidden = lax.dot_general(scaled, w_down, cols_last, preferred_element_type=jnp.float32)
    d_up = (d_hidden * swish).astype(jnp.bfloat16)
    d_gate = (d_hidden * pre_up * sigma * (1.0 + pre_gate * (1.0 - sigma))).astype(jnp.bfloat16)
    back = lax.dot_general(d_gate, w_gate, cols_last, preferred_element_type=jnp.float32)
    back = (
        back + lax.dot_general(d_up, w_up, cols_last, preferred_element_type=jnp.float32)
    ).astype(jnp.bfloat16)
    returned = lax.all_to_all(
        back.reshape(owners, CAP, width), "ep", split_axis=0, concat_axis=0, tiled=True
    ).reshape(owners * CAP, width)
    input_grad = lax.dot_general(
        dispatch, returned, rows_first, preferred_element_type=jnp.float32
    ).astype(jnp.bfloat16)
    units_all = lax.all_gather(
        jnp.concatenate([d_gate, d_up, hidden], axis=1), "rep", axis=0, tiled=True
    )
    both = lax.dot_general(
        rows_own, units_all[:, : 2 * units], rows_first, preferred_element_type=jnp.float32
    ) / groups
    gate_grad = both[:, :units]
    up_grad = both[:, units:]
    hidden_all = units_all[:, 2 * units :]
    share = width // groups
    scaled_own = lax.dynamic_slice_in_dim(scaled_all, lax.axis_index("rep") * share, share, axis=1)
    form = small_rows if groups * rows < units else small_units
    down_update = form(scaled_own, scaled_all, hidden_all, groups)
    return (input_grad, gate_grad[None], up_grad[None], down_update[None])


def solution(mesh):
    in_specs = (
        P(("rep", "ep"), None),
        P(("rep", "ep"), None),
        P(("rep", "ep"), None),
        P(("rep", "ep"), None),
        P("ep", None, None),
        P("ep", None, None),
        P("ep", None, None),
    )
    out_specs = (
        P(("rep", "ep"), None),
        P("ep", "rep", None),
        P("ep", "rep", None),
        P("ep", "rep", None),
    )
    return jax.shard_map(
        per_device, mesh=mesh, in_specs=in_specs, out_specs=out_specs, check_vma=False
    )
```
